32 devices in a mesh: prow: 4 (over y, x), pcol: 8 (over z, core).
Axes of the slice: x: 2, y: 2, z: 4, core: 2. Of those that a mesh axis runs over, the one named last changes fastest.
Arguments:
- matrix: float32 [2, 14336, 14336], P(None, 'pcol', 'prow'), may hold values from -6 to 6
- panel_lower: float32 [2, 64, 14336], P(None, None, ('prow', 'pcol')), may hold values from -0.75 to 0.75
- pivot_rows: int32 [64], replicated, may hold values from 0 to 14335, as said below
Outputs:
- updated: float32 [2, 14336, 14336], P(None, 'pcol', 'prow')
The draws below stay inside these ranges and needn't reach their ends.
Inputs may be any that keep to these rules, and one draw needn't show every extreme that they name: pivot_rows[k] lies between k and 14335; some entry equals 14335.
All inputs are finite; a program needn't handle non-finite values.
Results may differ from the reference program's by a relative error of at most 0.0001.
Values sent between devices are 32-bit elements; how exact they have to be, the bound alone decides.
A program may use at most 320 MiB of HBM per device.

```python
import jax
import jax.numpy as jnp
from jax import lax

M = 14336
NB = 64


def draw_pivot_rows(key, part):
    start = jnp.arange(NB, dtype=jnp.int32)
    spread = jax.random.randint(key, (NB,), 0, M, dtype=jnp.int32)
    chosen = start + spread % (M - start)
    forced = jax.random.randint(jax.random.fold_in(key, 7), (), 0, NB, dtype=jnp.int32)
    return jnp.where(start == forced, M - 1, chosen).astype(jnp.int32)


def block_scale(key, extent, shards, least, top_value):
    level = 1.0
    for dim, shards_of in shards:
        steps = jax.random.uniform(jax.random.fold_in(jax.random.fold_in(key, 6), dim), (shards_of,), jnp.float32, least / len(shards), top_value / len(shards))
        level = level * jnp.repeat(jnp.exp(steps), extent[dim] // shards_of).reshape((-1,) + (1,) * (len(extent) - 1 - dim))
    return level


def gaussian(own_key, shape, scale, bound, shards=(), kind=jnp.bfloat16):
    result = jax.random.normal(own_key, shape, jnp.float32) * scale
    if len(shards) > 0:
        result = block_scale(own_key, shape, shards, -0.22, 0.18) * result
    return jnp.clip(result, min=-bound, max=bound).astype(kind)


def setup_inputs(seed: int = 0) -> dict:
    seeds = jax.random.split(jax.random.key(seed), 4)
    matrix = gaussian(seeds[0], (2, M, M), 1.0, 6.0, ((1, 8), (2, 4)), jnp.float32)
    panel_lower = gaussian(seeds[1], (2, NB, M), NB ** -0.5, 0.75, ((2, 32),), jnp.float32)
    pivot_rows = draw_pivot_rows(jax.random.fold_in(seeds[3], 71), 0)
    return dict(matrix=matrix, panel_lower=panel_lower, pivot_rows=pivot_rows)


def precise(left, right):
    return jnp.dot(left, right, precision=lax.Precision.HIGHEST, preferred_element_type=jnp.float32)


def complex_product(left, right):
    real_part = precise(left[0], right[0]) - precise(left[1], right[1])
    imag_part = precise(left[0], right[1]) + precise(left[1], right[0])
    return jnp.stack([real_part, imag_part])


def unit_lower_inverse(block):
    width = block.shape[1]
    strict = block * jnp.tril(jnp.ones((width, width), jnp.float32), -1)[None]
    ident = jnp.stack([jnp.eye(width, dtype=jnp.float32), jnp.zeros((width, width), jnp.float32)])
    inverse = ident - strict
    power = strict
    for section in range(1, max(1, (width - 1).bit_length())):
        power = complex_product(power, power)
        inverse = complex_product(inverse, ident + power)
    return inverse


def apply_swaps(pivot_rows, length):
    def one_swap(position, order_map):
        target = pivot_rows[position]
        first = order_map[position]
        second = order_map[target]
        return order_map.at[position].set(second).at[target].set(first)
    return lax.fori_loop(0, pivot_rows.shape[0], one_swap, jnp.arange(length, dtype=jnp.int32))


def reference(matrix, panel_lower, pivot_rows):
    order_map = apply_swaps(pivot_rows, M)
    swapped = jnp.take(matrix, order_map, axis=2)
    lower_diag = jnp.swapaxes(panel_lower[:, :, :NB], 1, 2)
    inverse = unit_lower_inverse(lower_diag)
    upper = complex_product(swapped[:, :, :NB], jnp.swapaxes(inverse, 1, 2))
    below = swapped[:, :, NB:] - complex_product(upper, panel_lower[:, :, NB:])
    return jnp.concatenate([upper, below], axis=2)
```

```python
import jax
import jax.numpy as jnp
from jax import lax
from jax.experimental import pallas as pl
from jax.experimental.pallas import tpu as pltpu
from jax.sharding import PartitionSpec as P

LANES = 128
MIB = 1 << 20


def largest_divisor(extent, limit, multiple):
    size = multiple
    for candidate in range(multiple, limit + 1, multiple):
        if extent % candidate == 0:
            size = candidate
    return size


def precise(left, right):
    return jnp.dot(left, right, precision=lax.Precision.HIGHEST, preferred_element_type=jnp.float32)


def displaced_rows(pivot_col):
    width = pivot_col.shape[0]
    step = lax.broadcasted_iota(jnp.int32, (width, LANES), 0)
    lane = lax.broadcasted_iota(jnp.int32, (width, LANES), 1)
    earlier = jnp.where((pivot_col == lane) & (step < lane), step, -1)
    latest = jnp.max(earlier, axis=0, keepdims=True)
    latest = jnp.where(latest < 0, lane[:1], latest)
    chain = jnp.broadcast_to(latest, (8, LANES))
    for _ in range(max(1, (width - 1).bit_length())):
        chain = jnp.take_along_axis(chain, chain, axis=1)
    return chain


def wanted_rows(pivot_row, pivot_col):
    width = pivot_col.shape[0]
    step = lax.broadcasted_iota(jnp.int32, (width, LANES), 0)
    lane = lax.broadcasted_iota(jnp.int32, (width, LANES), 1)
    chain = displaced_rows(pivot_col)
    earlier = jnp.where((pivot_col == pivot_row) & (step < lane), step, -1)
    latest = jnp.broadcast_to(jnp.max(earlier, axis=0, keepdims=True), (8, LANES))
    from_chain = jnp.take_along_axis(chain, jnp.maximum(latest, 0), axis=1)
    top = jnp.where(latest < 0, jnp.broadcast_to(pivot_row, (8, LANES)), from_chain)
    lane8 = lax.broadcasted_iota(jnp.int32, (8, LANES), 1)
    return jnp.where(lane8 < width, top, lane8 - width)


def pick_kernel(pivot_row_ref, pivot_col_ref, matrix_ref, picked_ref):
    row_count = matrix_ref.shape[2]
    column_count = matrix_ref.shape[1]
    base = lax.axis_index("prow") * row_count
    local = wanted_rows(pivot_row_ref[...], pivot_col_ref[...]) - base
    owned = (local >= 0) & (local < row_count)
    tile = jnp.where(owned, local // LANES, -1)
    within = jnp.where(owned, local % LANES, 0)
    group = 16
    tile = jnp.concatenate([tile] * (group // 8), axis=0)
    within = jnp.concatenate([within] * (group // 8), axis=0)

    def one_group(g, carry):
        rows = pl.ds(pl.multiple_of(g * group, group), group)
        for part in range(2):
            total = jnp.zeros((group, LANES), jnp.float32)
            for t in range(row_count // LANES):
                block = matrix_ref[part, rows, pl.ds(t * LANES, LANES)]
                total = jnp.where(tile == t, jnp.take_along_axis(block, within, axis=1), total)
            picked_ref[part, rows, :] = total
        return carry

    lax.fori_loop(0, column_count // group, one_group, 0)


def pick(pivot_row, pivot_col, matrix):
    _, columns, rows = matrix.shape
    chunk = largest_divisor(columns, 128, 16)
    return pl.pallas_call(
        pick_kernel,
        out_shape=jax.ShapeDtypeStruct((2, columns, LANES), jnp.float32),
        grid=(columns // chunk,),
        in_specs=[
            pl.BlockSpec(pivot_row.shape, lambda i: (0, 0)),
            pl.BlockSpec(pivot_col.shape, lambda i: (0, 0)),
            pl.BlockSpec((2, chunk, rows), lambda i: (0, i, 0)),
        ],
        out_specs=pl.BlockSpec((2, chunk, LANES), lambda i: (0, i, 0)),
        compiler_params=pltpu.CompilerParams(vmem_limit_bytes=24 * MIB),
        cost_estimate=pl.CostEstimate(flops=columns * rows * 2, bytes_accessed=columns * rows * 8, transcendentals=0),
    )(pivot_row, pivot_col, matrix)


def split(value):
    high = value.astype(jnp.bfloat16)
    return high, (value - high.astype(jnp.float32)).astype(jnp.bfloat16)


def prepare_kernel(pivot_col_ref, slab_ref, corner_ref, panel_ref, left_ref, right_ref, keep_ref):
    width = panel_ref.shape[1]
    row_count = panel_ref.shape[2]
    base = lax.axis_index("prow") * row_count
    up = lax.broadcasted_iota(jnp.int32, (width, width), 0) < lax.broadcasted_iota(jnp.int32, (width, width), 1)
    real = jnp.where(up, corner_ref[0], 0.0)
    imag = jnp.where(up, corner_ref[1], 0.0)
    power = jnp.concatenate(
        [jnp.concatenate([real, imag], axis=1), jnp.concatenate([-imag, real], axis=1)], axis=0
    )
    ident = (
        lax.broadcasted_iota(jnp.int32, power.shape, 0) == lax.broadcasted_iota(jnp.int32, power.shape, 1)
    ).astype(jnp.float32)
    inverse = ident - power
    for _ in range(1, max(1, (width - 1).bit_length())):
        power = precise(power, power)
        inverse = precise(inverse, ident + power)

    chunk = largest_divisor(slab_ref.shape[1], 256, 16)

    def one_chunk(g, carry):
        rows = pl.ds(pl.multiple_of(g * chunk, chunk), chunk)
        parts = [slab_ref[part, rows, :] for part in range(2)]
        top = jnp.concatenate([part[:, :width] for part in parts], axis=1)
        upper_high, upper_low = split(precise(top, inverse))
        left_ref[rows, 0:LANES] = upper_high
        left_ref[rows, LANES : 2 * LANES] = upper_low
        for part in range(2):
            start = (2 + 2 * part) * LANES
            high, low = split(parts[part][:, width:])
            left_ref[rows, start : start + LANES] = upper_high
            left_ref[rows, start + LANES : start + 2 * LANES] = jnp.concatenate([high, low], axis=1)
        return carry

    lax.fori_loop(0, slab_ref.shape[1] // chunk, one_chunk, 0)

    chain = displaced_rows(pivot_col_ref[...])[:1]
    source_is = (
        (lax.broadcasted_iota(jnp.int32, (width, width), 0) == chain[:, :width])
        .astype(jnp.float32)
        .astype(jnp.bfloat16)
    )
    span = largest_divisor(row_count, 512, LANES)

    def one_span(t, carry):
        start = pl.multiple_of(t * span, span)
        lanes = pl.ds(start, span)
        step = lax.broadcasted_iota(jnp.int32, (width, span), 0)
        position = lax.broadcasted_iota(jnp.int32, (width, span), 1) + (start + base)
        latest = jnp.max(jnp.where(pivot_col_ref[...] == position, step, -1), axis=0, keepdims=True)
        at_top = position < width
        moved = (latest == step) & jnp.logical_not(at_top)
        chosen = jnp.dot(
            source_is, moved.astype(jnp.float32).astype(jnp.bfloat16), preferred_element_type=jnp.float32
        ).astype(jnp.bfloat16)
        real = jnp.where(at_top, -(position == step).astype(jnp.float32), panel_ref[0, :, lanes])
        imag = jnp.where(at_top, 0.0, panel_ref[1, :, lanes])
        real_high, real_low = split(real)
        imag_high, imag_low = split(imag)
        for part in range(2):
            if part == 0:
                high = [-real_high, imag_high]
                low = [-real_low, imag_low]
            else:
                high = [-imag_high, -real_high]
                low = [-imag_low, -real_low]
            for index, piece in enumerate(high + high + low + [chosen, chosen]):
                right_ref[part, index * width : (index + 1) * width, lanes] = piece
        keep = (latest < 0) & (position[:1] >= width)
        keep_ref[:, lanes] = jnp.broadcast_to(keep.astype(jnp.float32), (8, span))
        return carry

    lax.fori_loop(0, row_count // span, one_span, 0)


def prepare(pivot_col, slab, corner, panel):
    _, columns, _ = slab.shape
    _, width, rows = panel.shape
    whole = pl.BlockSpec(memory_space=pltpu.VMEM)
    return pl.pallas_call(
        prepare_kernel,
        out_shape=(
            jax.ShapeDtypeStruct((columns, 6 * LANES), jnp.bfloat16),
            jax.ShapeDtypeStruct((2, 8 * width, rows), jnp.bfloat16),
            jax.ShapeDtypeStruct((8, rows), jnp.float32),
        ),
        in_specs=[whole] * 4,
        out_specs=(whole,) * 3,
        compiler_params=pltpu.CompilerParams(vmem_limit_bytes=28 * MIB),
    )(pivot_col, slab, corner, panel)


def update_kernel(left_ref, right_ref, keep_ref, matrix_ref, out_ref):
    columns, rows = matrix_ref.shape[1:]
    half = 2 * LANES
    span = largest_divisor(rows, 256, LANES)
    offset = pl.program_id(1) * rows

    def one_span(t, carry):
        here = pl.ds(pl.multiple_of(t * span, span), span)
        there = pl.ds(pl.multiple_of(offset + t * span, LANES), span)
        keep = keep_ref[:1, there] > 0.5
        for part in range(2):
            product = jnp.dot(
                left_ref[:, 0:half], right_ref[part, 0:half, there], preferred_element_type=jnp.float32
            ) + jnp.dot(
                left_ref[:, (1 + part) * half : (2 + part) * half],
                right_ref[part, half : 2 * half, there],
                preferred_element_type=jnp.float32,
            )
            out_ref[part, :, here] = jnp.where(keep, matrix_ref[part, :, here], 0.0) + product
        return carry

    lax.fori_loop(0, rows // span, one_span, 0)


def update(left, right, keep, matrix):
    _, columns, rows = matrix.shape
    chunk = largest_divisor(columns, 256, 16)
    row_chunk = largest_divisor(rows, 1792, LANES)
    return pl.pallas_call(
        update_kernel,
        out_shape=jax.ShapeDtypeStruct(matrix.shape, jnp.float32),
        grid=(columns // chunk, rows // row_chunk),
        in_specs=[
            pl.BlockSpec((chunk, left.shape[1]), lambda i, j: (i, 0)),
            pl.BlockSpec(right.shape, lambda i, j: (0, 0, 0), pipeline_mode=pl.Buffered(1)),
            pl.BlockSpec(keep.shape, lambda i, j: (0, 0), pipeline_mode=pl.Buffered(1)),
            pl.BlockSpec((2, chunk, row_chunk), lambda i, j: (0, i, j)),
        ],
        out_specs=pl.BlockSpec((2, chunk, row_chunk), lambda i, j: (0, i, j)),
        compiler_params=pltpu.CompilerParams(vmem_limit_bytes=40 * MIB),
    )(left, right, keep, matrix)


def on_device(matrix, panel_lower, pivot_rows):
    width = pivot_rows.shape[0]
    pivot_row = jnp.pad(pivot_rows, (0, LANES - width), constant_values=-1).reshape(1, LANES)
    pivot_col = pivot_rows.reshape(width, 1)
    gathered = lax.all_gather(panel_lower, "pcol", axis=2, tiled=True)
    corner = lax.psum(jnp.where(lax.axis_index("prow") == 0, gathered[:, :, :width], 0.0), "prow")
    picked = pick(pivot_row, pivot_col, matrix)
    slab = lax.psum(picked, "prow")
    left, right, keep = prepare(pivot_col, slab, corner, gathered)
    return update(left, right, keep, matrix)


def solution(mesh):
    return jax.shard_map(
        on_device,
        mesh=mesh,
        in_specs=(P(None, "pcol", "prow"), P(None, None, ("prow", "pcol")), P()),
        out_specs=P(None, "pcol", "prow"),
        check_vma=False,
    )
```

```python
import jax
import jax.numpy as jnp
from jax import lax
from jax.experimental import pallas as pl
from jax.experimental.pallas import tpu as pltpu
from jax.sharding import PartitionSpec as P

LANES = 128
MIB = 1 << 20


def largest_divisor(extent, limit, multiple):
    size = multiple
    for candidate in range(multiple, limit + 1, multiple):
        if extent % candidate == 0:
            size = candidate
    return size


def precise(left, right):
    return jnp.dot(left, right, precision=lax.Precision.HIGHEST, preferred_element_type=jnp.float32)


def displaced_rows(pivot_col):
    width = pivot_col.shape[0]
    step = lax.broadcasted_iota(jnp.int32, (width, LANES), 0)
    lane = lax.broadcasted_iota(jnp.int32, (width, LANES), 1)
    earlier = jnp.where((pivot_col == lane) & (step < lane), step, -1)
    latest = jnp.max(earlier, axis=0, keepdims=True)
    latest = jnp.where(latest < 0, lane[:1], latest)
    chain = jnp.broadcast_to(latest, (8, LANES))
    for _ in range(max(1, (width - 1).bit_length())):
        chain = jnp.take_along_axis(chain, chain, axis=1)
    return chain


def wanted_rows(pivot_row, pivot_col):
    width = pivot_col.shape[0]
    step = lax.broadcasted_iota(jnp.int32, (width, LANES), 0)
    lane = lax.broadcasted_iota(jnp.int32, (width, LANES), 1)
    chain = displaced_rows(pivot_col)
    earlier = jnp.where((pivot_col == pivot_row) & (step < lane), step, -1)
    latest = jnp.broadcast_to(jnp.max(earlier, axis=0, keepdims=True), (8, LANES))
    from_chain = jnp.take_along_axis(chain, jnp.maximum(latest, 0), axis=1)
    top = jnp.where(latest < 0, jnp.broadcast_to(pivot_row, (8, LANES)), from_chain)
    lane8 = lax.broadcasted_iota(jnp.int32, (8, LANES), 1)
    return jnp.where(lane8 < width, top, lane8 - width)


def pick_kernel(pivot_row_ref, pivot_col_ref, matrix_ref, picked_ref):
    row_count = matrix_ref.shape[2]
    column_count = matrix_ref.shape[1]
    base = lax.axis_index("prow") * row_count
    local = wanted_rows(pivot_row_ref[...], pivot_col_ref[...]) - base
    owned = (local >= 0) & (local < row_count)
    tile = jnp.where(owned, local // LANES, -1)
    within = jnp.where(owned, local % LANES, 0)
    group = 16
    tile = jnp.concatenate([tile] * (group // 8), axis=0)
    within = jnp.concatenate([within] * (group // 8), axis=0)

    def one_group(g, carry):
        rows = pl.ds(pl.multiple_of(g * group, group), group)
        for part in range(2):
            total = jnp.zeros((group, LANES), jnp.float32)
            for t in range(row_count // LANES):
                block = matrix_ref[part, rows, pl.ds(t * LANES, LANES)]
                total = jnp.where(tile == t, jnp.take_along_axis(block, within, axis=1), total)
            picked_ref[part, rows, :] = total
        return carry

    lax.fori_loop(0, column_count // group, one_group, 0)


def pick(pivot_row, pivot_col, matrix):
    _, columns, rows = matrix.shape
    chunk = largest_divisor(columns, 128, 16)
    return pl.pallas_call(
        pick_kernel,
        out_shape=jax.ShapeDtypeStruct((2, columns, LANES), jnp.float32),
        grid=(columns // chunk,),
        in_specs=[
            pl.BlockSpec(pivot_row.shape, lambda i: (0, 0)),
            pl.BlockSpec(pivot_col.shape, lambda i: (0, 0)),
            pl.BlockSpec((2, chunk, rows), lambda i: (0, i, 0)),
        ],
        out_specs=pl.BlockSpec((2, chunk, LANES), lambda i: (0, i, 0)),
        compiler_params=pltpu.CompilerParams(vmem_limit_bytes=24 * MIB),
        cost_estimate=pl.CostEstimate(flops=columns * rows * 2, bytes_accessed=columns * rows * 8, transcendentals=0),
    )(pivot_row, pivot_col, matrix)


def split(value):
    high = value.astype(jnp.bfloat16)
    return high, (value - high.astype(jnp.float32)).astype(jnp.bfloat16)


def prepare_kernel(pivot_col_ref, top_ref, old_ref, corner_ref, panel_ref, left_ref, right_ref, keep_ref):
    slots, _, width, share = panel_ref.shape
    row_count = slots * share
    base = lax.axis_index("prow") * row_count
    up = lax.broadcasted_iota(jnp.int32, (width, width), 0) < lax.broadcasted_iota(jnp.int32, (width, width), 1)
    real = jnp.where(up, corner_ref[:, :width], 0.0)
    imag = jnp.where(up, corner_ref[:, width:], 0.0)
    power = jnp.concatenate(
        [jnp.concatenate([real, imag], axis=1), jnp.concatenate([-imag, real], axis=1)], axis=0
    )
    ident = (
        lax.broadcasted_iota(jnp.int32, power.shape, 0) == lax.broadcasted_iota(jnp.int32, power.shape, 1)
    ).astype(jnp.float32)
    inverse = ident - power
    for _ in range(1, max(1, (width - 1).bit_length())):
        power = precise(power, power)
        inverse = precise(inverse, ident + power)

    chunk = largest_divisor(top_ref.shape[0], 256, 16)

    def one_chunk(g, carry):
        rows = pl.ds(pl.multiple_of(g * chunk, chunk), chunk)
        upper_high, upper_low = split(precise(top_ref[rows, :], inverse))
        old_high, old_low = split(old_ref[rows, :])
        for part in range(2):
            mine = slice(part * width, (part + 1) * width)
            left_ref[part, rows, 0:LANES] = upper_high
            left_ref[part, rows, LANES : 2 * LANES] = upper_low
            left_ref[part, rows, 2 * LANES : 3 * LANES] = upper_high
            left_ref[part, rows, 3 * LANES : 4 * LANES] = jnp.concatenate(
                [old_high[:, mine], old_low[:, mine]], axis=1
            )
        return carry

    lax.fori_loop(0, top_ref.shape[0] // chunk, one_chunk, 0)

    chain = displaced_rows(pivot_col_ref[...])[:1]
    source_is = (
        (lax.broadcasted_iota(jnp.int32, (width, width), 0) == chain[:, :width])
        .astype(jnp.float32)
        .astype(jnp.bfloat16)
    )
    group = 1
    while group < slots and (group * share) % LANES:
        group *= 2
    span = group * share

    for t in range(slots // group):
        lanes = slice(t * span, (t + 1) * span)
        step = lax.broadcasted_iota(jnp.int32, (width, span), 0)
        position = lax.broadcasted_iota(jnp.int32, (width, span), 1) + (t * span + base)
        latest = jnp.max(jnp.where(pivot_col_ref[...] == position, step, -1), axis=0, keepdims=True)
        at_top = position < width
        moved = (latest == step) & jnp.logical_not(at_top)
        chosen = jnp.dot(
            source_is, moved.astype(jnp.float32).astype(jnp.bfloat16), preferred_element_type=jnp.float32
        ).astype(jnp.bfloat16)
        pieces = [
            jnp.concatenate([panel_ref[t * group + g, part] for g in range(group)], axis=1) for part in range(2)
        ]
        real = jnp.where(at_top, -(position == step).astype(jnp.float32), pieces[0])
        imag = jnp.where(at_top, 0.0, pieces[1])
        real_high, real_low = split(real)
        imag_high, imag_low = split(imag)
        for part in range(2):
            if part == 0:
                high = [-real_high, imag_high]
                low = [-real_low, imag_low]
            else:
                high = [-imag_high, -real_high]
                low = [-imag_low, -real_low]
            for index, piece in enumerate(high + high + low + [chosen, chosen]):
                right_ref[part, index * width : (index + 1) * width, lanes] = piece
        keep = (latest < 0) & (position[:1] >= width)
        keep_ref[:, lanes] = jnp.broadcast_to(keep.astype(jnp.float32), (8, span))


def prepare(pivot_col, top, old, corner, panel):
    columns = top.shape[0]
    slots, _, width, share = panel.shape
    rows = slots * share
    whole = pl.BlockSpec(memory_space=pltpu.VMEM)
    return pl.pallas_call(
        prepare_kernel,
        out_shape=(
            jax.ShapeDtypeStruct((2, columns, 4 * LANES), jnp.bfloat16),
            jax.ShapeDtypeStruct((2, 8 * width, rows), jnp.bfloat16),
            jax.ShapeDtypeStruct((8, rows), jnp.float32),
        ),
        in_specs=[whole] * 5,
        out_specs=(whole,) * 3,
        compiler_params=pltpu.CompilerParams(vmem_limit_bytes=32 * MIB),
    )(pivot_col, top, old, corner, panel)


def update_kernel(left_ref, right_ref, keep_ref, matrix_ref, out_ref):
    columns = matrix_ref.shape[1]
    chunk = largest_divisor(columns, 896, 16)
    keep = keep_ref[:1, :] > 0.5
    for part in range(2):
        for start in range(0, columns, chunk):
            rows = slice(start, start + chunk)
            product = jnp.dot(left_ref[part, rows, :], right_ref[part], preferred_element_type=jnp.float32)
            out_ref[part, rows, :] = jnp.where(keep, matrix_ref[part, rows, :], 0.0) + product


def update(left, right, keep, matrix):
    _, columns, rows = matrix.shape
    span = largest_divisor(rows, 2 * LANES, LANES)
    return pl.pallas_call(
        update_kernel,
        out_shape=jax.ShapeDtypeStruct(matrix.shape, jnp.float32),
        grid=(rows // span,),
        in_specs=[
            pl.BlockSpec(left.shape, lambda j: (0, 0, 0), pipeline_mode=pl.Buffered(1)),
            pl.BlockSpec((2, right.shape[1], span), lambda j: (0, 0, j)),
            pl.BlockSpec((8, span), lambda j: (0, j)),
            pl.BlockSpec((2, columns, span), lambda j: (0, 0, j)),
        ],
        out_specs=pl.BlockSpec((2, columns, span), lambda j: (0, 0, j)),
        compiler_params=pltpu.CompilerParams(vmem_limit_bytes=40 * MIB),
    )(left, right, keep, matrix)


def exchange_kernel(
    peers, ring, pivot_row_ref, pivot_col_ref, corner_ref, panel_ref, matrix_ref,
    top_ref, old_ref, corner_out_ref, slots_ref,
    choose, mine, old, inbox, total,
    rs_send, rs_recv, ag_send, ag_recv, old_send, old_recv, spread_send, spread_recv,
    panel_send, panel_recv, pass_send, pass_recv, corner_send, corner_recv, local_sem,
):
    width = pivot_col_ref.shape[0]
    _, chunk, row_count = matrix_ref.shape
    quarter = chunk // peers
    last = pl.num_programs(0) - 1
    step = pl.program_id(0)
    p = lax.axis_index("prow")
    q = lax.axis_index("pcol")
    sibling = q + 1 - 2 * lax.rem(q, 2)
    hops = ring // 2

    def other(d):
        return lax.rem(p + d, peers)

    def sender(d):
        return lax.rem(p + peers - d, peers)

    def along(d):
        return lax.rem(q + 2 * d, ring)

    def behind(d):
        return lax.rem(q + ring - 2 * d, ring)

    def remote(src, dst, send, recv, row, column):
        return pltpu.make_async_remote_copy(
            src_ref=src, dst_ref=dst, send_sem=send, recv_sem=recv,
            device_id=(row, column), device_id_type=pl.DeviceIdType.MESH,
        )

    def part_rows(i, owner):
        return pl.ds(pl.multiple_of(i * chunk + owner * quarter, quarter), quarter)

    def scatter_copy(i, d):
        return remote(
            mine.at[part_rows(i, other(d))], inbox.at[i, d - 1], rs_send.at[i, d - 1], rs_recv.at[i, d - 1], other(d), q
        )

    def gather_copy(i, d, owner):
        return remote(
            total.at[i], top_ref.at[part_rows(i, owner)], ag_send.at[i, d - 1], ag_recv.at[i, d - 1], other(d), q
        )

    def old_copy(i, d, target):
        return remote(
            old.at[part_rows(i, target)], old_ref.at[part_rows(i, target)], old_send.at[i, d - 1], old_recv.at[i], other(d), q
        )

    def spread_root(i, d):
        return remote(
            old.at[part_rows(i, 0)], old_ref.at[part_rows(i, 0)], spread_send.at[i, d - 1], spread_recv.at[i, d - 1], other(d), q
        )

    def spread_copy(i, d, owner):
        return remote(
            old_ref.at[part_rows(i, owner)], old_ref.at[part_rows(i, owner)],
            spread_send.at[i, d - 1], spread_recv.at[i, d - 1], other(d), q,
        )

    def panel_copy(d, owner):
        return remote(panel_ref, slots_ref.at[owner], panel_send.at[d], panel_recv.at[d], p, along(d))

    def sibling_copy():
        return remote(panel_ref, slots_ref.at[q], panel_send.at[0], panel_recv.at[0], p, sibling)

    def pass_copy(d, owner):
        return remote(slots_ref.at[owner], slots_ref.at[owner], pass_send.at[d], pass_recv.at[d], p, sibling)

    def corner_down(d):
        return remote(corner_ref, corner_out_ref, corner_send.at[d - 1], corner_recv.at[0], other(d), q)

    def corner_across(d):
        return remote(
            corner_ref, corner_out_ref, corner_send.at[peers + d - 1], corner_recv.at[0], p, lax.rem(q + d, ring)
        )

    def corner_forward(d):
        return remote(
            corner_out_ref, corner_out_ref, corner_send.at[peers + d - 1], corner_recv.at[0], p, lax.rem(q + d, ring)
        )

    def own_panel():
        return pltpu.make_async_copy(panel_ref, slots_ref.at[q], local_sem.at[0])

    def own_corner():
        return pltpu.make_async_copy(corner_ref, corner_out_ref, local_sem.at[1])

    def own_old():
        return pltpu.make_async_copy(old, old_ref, local_sem.at[2])

    def own_total(i):
        return pltpu.make_async_copy(total.at[i], top_ref.at[part_rows(i, p)], local_sem.at[3 + i])

    @pl.when(step == 0)
    def _():
        barrier = pltpu.get_barrier_semaphore()
        for d in range(1, peers):
            pl.semaphore_signal(barrier, inc=1, device_id=(other(d), q), device_id_type=pl.DeviceIdType.MESH)
        for d in range(1, ring):
            pl.semaphore_signal(
                barrier, inc=1, device_id=(p, lax.rem(q + d, ring)), device_id_type=pl.DeviceIdType.MESH
            )
        pl.semaphore_wait(barrier, peers + ring - 2)
        for d in range(1, hops):
            panel_copy(d, q).start()
        sibling_copy().start()
        own_panel().start()

        @pl.when((p == 0) & (q == 0))
        def _():
            for d in range(1, peers):
                corner_down(d).start()
            for d in range(1, ring):
                corner_across(d).start()
            own_corner().start()

        wanted = wanted_rows(pivot_row_ref[...], pivot_col_ref[...])[:1] - p * row_count
        wanted = jnp.concatenate([wanted[:, :width], wanted[:, :width]], axis=1)
        row = lax.broadcasted_iota(jnp.int32, choose.shape, 0)
        choose[...] = (row == wanted).astype(jnp.float32).astype(jnp.bfloat16)

    here = pl.ds(pl.multiple_of(step * chunk, chunk), chunk)
    found = []
    for part in range(2):
        high, low = split(matrix_ref[part])
        found.append(
            jnp.dot(high, choose[...], preferred_element_type=jnp.float32)
            + jnp.dot(low, choose[...], preferred_element_type=jnp.float32)
        )
    lane = lax.broadcasted_iota(jnp.int32, (chunk, LANES), 1)
    mine[here, :] = jnp.where(lane < width, found[0], found[1])
    for d in range(1, peers):
        scatter_copy(step, d).start()

    @pl.when(p == 0)
    def _():
        old[here, :] = jnp.concatenate([matrix_ref[0, :, :width], matrix_ref[1, :, :width]], axis=1)
        for d in range(1, peers):
            old_copy(step, d, d).start()
        for d in range(1, peers):
            spread_root(step, d).start()

    def finish(i):
        for d in range(1, peers):
            scatter_copy(i, d).wait_recv()
        summed = mine[part_rows(i, p), :]
        for d in range(1, peers):
            summed = summed + inbox[i, d - 1]
        total[i] = summed
        for d in range(1, peers):
            gather_copy(i, d, p).start()
        own_total(i).start()

        @pl.when(p != 0)
        def _():
            old_copy(i, 1, p).wait_recv()
            for d in range(1, peers):
                @pl.when(other(d) != 0)
                def _(d=d):
                    spread_copy(i, d, p).start()

    @pl.when(step > 0)
    def _():
        finish(step - 1)

    @pl.when(step == last)
    def _():
        for d in range(1, hops):
            panel_copy(d, behind(d)).wait_recv()
            pass_copy(d, behind(d)).start()

        @pl.when((q == 0) & (p != 0))
        def _():
            corner_down(1).wait_recv()
            for d in range(1, ring):
                corner_forward(d).start()

        finish(last)

        @pl.when(p == 0)
        def _():
            own_old().start()
            own_old().wait()

        @pl.when((p == 0) & (q == 0))
        def _():
            own_corner().wait()
            for d in range(1, peers):
                corner_down(d).wait_send()
            for d in range(1, ring):
                corner_across(d).wait_send()

        @pl.when((p != 0) & (q == 0))
        def _():
            for d in range(1, ring):
                corner_forward(d).wait_send()

        @pl.when(q != 0)
        def _():
            corner_across(1).wait_recv()

        own_panel().wait()
        remote(panel_ref, slots_ref.at[sibling], panel_send.at[0], panel_recv.at[0], p, sibling).wait()
        for d in range(1, hops):
            panel_copy(d, q).wait_send()
            pass_copy(d, behind(d)).wait_send()
            pass_copy(d, lax.rem(sibling + ring - 2 * d, ring)).wait_recv()

        def drain(i, carry):
            own_total(i).wait()
            for d in range(1, peers):
                scatter_copy(i, d).wait_send()
                gather_copy(i, d, p).wait_send()
                gather_copy(i, d, sender(d)).wait_recv()

            @pl.when(p == 0)
            def _():
                for d in range(1, peers):
                    old_copy(i, d, d).wait_send()
                    spread_root(i, d).wait_send()

            @pl.when(p != 0)
            def _():
                for d in range(1, peers):
                    spread_copy(i, d, sender(d)).wait_recv()

                    @pl.when(other(d) != 0)
                    def _(d=d):
                        spread_copy(i, d, p).wait_send()

            return carry

        lax.fori_loop(0, last + 1, drain, 0)


def exchange(pivot_row, pivot_col, corner, panel, matrix, chunk):
    _, columns, rows = matrix.shape
    peers, ring = lax.axis_size("prow"), lax.axis_size("pcol")
    steps = columns // chunk
    quarter = chunk // peers
    anywhere = pl.BlockSpec(memory_space=pl.ANY)
    dma = pltpu.SemaphoreType.DMA
    return pl.pallas_call(
        lambda *refs: exchange_kernel(peers, ring, *refs),
        out_shape=(
            jax.ShapeDtypeStruct((columns, LANES), jnp.float32),
            jax.ShapeDtypeStruct((columns, LANES), jnp.float32),
            jax.ShapeDtypeStruct(corner.shape, jnp.float32),
            jax.ShapeDtypeStruct((ring,) + panel.shape, jnp.float32),
        ),
        grid=(steps,),
        in_specs=[
            pl.BlockSpec(pivot_row.shape, lambda i: (0, 0)),
            pl.BlockSpec(pivot_col.shape, lambda i: (0, 0)),
            anywhere,
            anywhere,
            pl.BlockSpec((2, chunk, rows), lambda i: (0, i, 0)),
        ],
        out_specs=(anywhere,) * 4,
        scratch_shapes=[
            pltpu.VMEM((rows, LANES), jnp.bfloat16),
            pltpu.VMEM((columns, LANES), jnp.float32),
            pltpu.VMEM((columns, LANES), jnp.float32),
            pltpu.VMEM((steps, peers - 1, quarter, LANES), jnp.float32),
            pltpu.VMEM((steps, quarter, LANES), jnp.float32),
            dma((steps, peers - 1)), dma((steps, peers - 1)),
            dma((steps, peers - 1)), dma((steps, peers - 1)),
            dma((steps, peers - 1)), dma((steps,)),
            dma((steps, peers - 1)), dma((steps, peers - 1)),
            dma((ring // 2,)), dma((ring // 2,)),
            dma((ring // 2,)), dma((ring // 2,)),
            dma((peers + ring,)), dma((1,)), dma((3 + steps,)),
        ],
        compiler_params=pltpu.CompilerParams(
            vmem_limit_bytes=44 * MIB, collective_id=0, has_side_effects=True
        ),
        cost_estimate=pl.CostEstimate(flops=columns * rows * 8 * LANES, bytes_accessed=columns * rows * 8, transcendentals=0),
    )(pivot_row, pivot_col, corner, panel, matrix)


def exchange_plain(pivot_row, pivot_col, corner, panel, matrix):
    width = panel.shape[1]
    slots = lax.all_gather(panel, "pcol")
    mine = (lax.axis_index("prow") == 0) & (lax.axis_index("pcol") == 0)
    share = panel.shape[2]
    if share < width:
        head = jnp.concatenate([slots[k] for k in range(-(-width // share))], axis=2)[:, :, :width]
        first = jnp.where(lax.axis_index("prow") == 0, head, 0.0)
        corner = lax.psum(first, "prow")
    else:
        corner = lax.psum(jnp.where(mine, panel[:, :, :width], 0.0), ("prow", "pcol"))
    corner = jnp.concatenate([corner[0], corner[1]], axis=1)
    slab = lax.psum(pick(pivot_row, pivot_col, matrix), "prow")
    top = jnp.concatenate([slab[0, :, :width], slab[1, :, :width]], axis=1)
    old = jnp.concatenate([slab[0, :, width:], slab[1, :, width:]], axis=1)
    slots = jnp.moveaxis(slots, 0, 2).reshape(1, 2, width, -1)
    return top, old, corner, slots


def on_device(matrix, panel_lower, pivot_rows):
    width = pivot_rows.shape[0]
    share = panel_lower.shape[2]
    columns = matrix.shape[1]
    peers, ring = lax.axis_size("prow"), lax.axis_size("pcol")
    pivot_row = jnp.pad(pivot_rows, (0, LANES - width), constant_values=-1).reshape(1, LANES)
    pivot_col = pivot_rows.reshape(width, 1)
    chunk = largest_divisor(columns, 256, 16)
    if share % width == 0 and ring <= 8 and chunk % (8 * peers) == 0:
        corner = jnp.concatenate([panel_lower[0, :, :width], panel_lower[1, :, :width]], axis=1)
        moved = exchange(pivot_row, pivot_col, corner, panel_lower, matrix, chunk)
    else:
        moved = exchange_plain(pivot_row, pivot_col, None, panel_lower, matrix)
    left, right, keep = prepare(pivot_col, *moved)
    return update(left, right, keep, matrix)


def solution(mesh):
    return jax.shard_map(
        on_device,
        mesh=mesh,
        in_specs=(P(None, "pcol", "prow"), P(None, None, ("prow", "pcol")), P()),
        out_specs=P(None, "pcol", "prow"),
        check_vma=False,
    )
```

```python
import jax
import jax.numpy as jnp
from jax import lax
from jax.experimental import pallas as pl
from jax.experimental.pallas import tpu as pltpu
from jax.sharding import PartitionSpec as P

LANES = 128
MIB = 1 << 20


def largest_divisor(extent, limit, multiple):
    size = multiple
    for candidate in range(multiple, limit + 1, multiple):
        if extent % candidate == 0:
            size = candidate
    return size


def precise(left, right):
    return jnp.dot(left, right, precision=lax.Precision.HIGHEST, preferred_element_type=jnp.float32)


def displaced_rows(pivot_col):
    width = pivot_col.shape[0]
    step = lax.broadcasted_iota(jnp.int32, (width, LANES), 0)
    lane = lax.broadcasted_iota(jnp.int32, (width, LANES), 1)
    earlier = jnp.where((pivot_col == lane) & (step < lane), step, -1)
    latest = jnp.max(earlier, axis=0, keepdims=True)
    latest = jnp.where(latest < 0, lane[:1], latest)
    chain = jnp.broadcast_to(latest, (8, LANES))
    for _ in range(max(1, (width - 1).bit_length())):
        chain = jnp.take_along_axis(chain, chain, axis=1)
    return chain


def wanted_rows(pivot_row, pivot_col):
    width = pivot_col.shape[0]
    step = lax.broadcasted_iota(jnp.int32, (width, LANES), 0)
    lane = lax.broadcasted_iota(jnp.int32, (width, LANES), 1)
    chain = displaced_rows(pivot_col)
    earlier = jnp.where((pivot_col == pivot_row) & (step < lane), step, -1)
    latest = jnp.broadcast_to(jnp.max(earlier, axis=0, keepdims=True), (8, LANES))
    from_chain = jnp.take_along_axis(chain, jnp.maximum(latest, 0), axis=1)
    top = jnp.where(latest < 0, jnp.broadcast_to(pivot_row, (8, LANES)), from_chain)
    lane8 = lax.broadcasted_iota(jnp.int32, (8, LANES), 1)
    return jnp.where(lane8 < width, top, lane8 - width)


def pick_kernel(pivot_row_ref, pivot_col_ref, matrix_ref, picked_ref):
    row_count = matrix_ref.shape[2]
    column_count = matrix_ref.shape[1]
    base = lax.axis_index("prow") * row_count
    local = wanted_rows(pivot_row_ref[...], pivot_col_ref[...]) - base
    owned = (local >= 0) & (local < row_count)
    tile = jnp.where(owned, local // LANES, -1)
    within = jnp.where(owned, local % LANES, 0)
    group = 16
    tile = jnp.concatenate([tile] * (group // 8), axis=0)
    within = jnp.concatenate([within] * (group // 8), axis=0)

    def one_group(g, carry):
        rows = pl.ds(pl.multiple_of(g * group, group), group)
        for part in range(2):
            total = jnp.zeros((group, LANES), jnp.float32)
            for t in range(row_count // LANES):
                block = matrix_ref[part, rows, pl.ds(t * LANES, LANES)]
                total = jnp.where(tile == t, jnp.take_along_axis(block, within, axis=1), total)
            picked_ref[part, rows, :] = total
        return carry

    lax.fori_loop(0, column_count // group, one_group, 0)


def pick(pivot_row, pivot_col, matrix):
    _, columns, rows = matrix.shape
    chunk = largest_divisor(columns, 128, 16)
    return pl.pallas_call(
        pick_kernel,
        out_shape=jax.ShapeDtypeStruct((2, columns, LANES), jnp.float32),
        grid=(columns // chunk,),
        in_specs=[
            pl.BlockSpec(pivot_row.shape, lambda i: (0, 0)),
            pl.BlockSpec(pivot_col.shape, lambda i: (0, 0)),
            pl.BlockSpec((2, chunk, rows), lambda i: (0, i, 0)),
        ],
        out_specs=pl.BlockSpec((2, chunk, LANES), lambda i: (0, i, 0)),
        compiler_params=pltpu.CompilerParams(vmem_limit_bytes=24 * MIB),
        cost_estimate=pl.CostEstimate(flops=columns * rows * 2, bytes_accessed=columns * rows * 8, transcendentals=0),
    )(pivot_row, pivot_col, matrix)


def split(value):
    high = value.astype(jnp.bfloat16)
    return high, (value - high.astype(jnp.float32)).astype(jnp.bfloat16)


def prepare_kernel(pivot_col_ref, top_ref, old_ref, corner_ref, panel_ref, left_ref, right_ref, keep_ref):
    slots, _, width, share = panel_ref.shape
    row_count = slots * share
    base = lax.axis_index("prow") * row_count
    up = lax.broadcasted_iota(jnp.int32, (width, width), 0) < lax.broadcasted_iota(jnp.int32, (width, width), 1)
    real = jnp.where(up, corner_ref[:, :width], 0.0)
    imag = jnp.where(up, corner_ref[:, width:], 0.0)
    power = jnp.concatenate(
        [jnp.concatenate([real, imag], axis=1), jnp.concatenate([-imag, real], axis=1)], axis=0
    )
    ident = (
        lax.broadcasted_iota(jnp.int32, power.shape, 0) == lax.broadcasted_iota(jnp.int32, power.shape, 1)
    ).astype(jnp.float32)
    inverse = ident - power
    for _ in range(1, max(1, (width - 1).bit_length())):
        power = precise(power, power)
        inverse = precise(inverse, ident + power)

    chunk = largest_divisor(top_ref.shape[0], 256, 16)

    def one_chunk(g, carry):
        rows = pl.ds(pl.multiple_of(g * chunk, chunk), chunk)
        upper_high, upper_low = split(precise(top_ref[rows, :], inverse))
        old_high, old_low = split(old_ref[rows, :])
        for part in range(2):
            mine = slice(part * width, (part + 1) * width)
            left_ref[part, rows, 0:LANES] = upper_high
            left_ref[part, rows, LANES : 2 * LANES] = upper_low
            left_ref[part, rows, 2 * LANES : 3 * LANES] = upper_high
            left_ref[part, rows, 3 * LANES : 4 * LANES] = jnp.concatenate(
                [old_high[:, mine], old_low[:, mine]], axis=1
            )
        return carry

    lax.fori_loop(0, top_ref.shape[0] // chunk, one_chunk, 0)

    chain = displaced_rows(pivot_col_ref[...])[:1]
    source_is = (
        (lax.broadcasted_iota(jnp.int32, (width, width), 0) == chain[:, :width])
        .astype(jnp.float32)
        .astype(jnp.bfloat16)
    )
    group = 1
    while group < slots and (group * share) % LANES:
        group *= 2
    span = group * share

    for t in range(slots // group):
        lanes = slice(t * span, (t + 1) * span)
        step = lax.broadcasted_iota(jnp.int32, (width, span), 0)
        position = lax.broadcasted_iota(jnp.int32, (width, span), 1) + (t * span + base)
        latest = jnp.max(jnp.where(pivot_col_ref[...] == position, step, -1), axis=0, keepdims=True)
        at_top = position < width
        moved = (latest == step) & jnp.logical_not(at_top)
        chosen = jnp.dot(
            source_is, moved.astype(jnp.float32).astype(jnp.bfloat16), preferred_element_type=jnp.float32
        ).astype(jnp.bfloat16)
        pieces = [
            jnp.concatenate([panel_ref[t * group + g, part] for g in range(group)], axis=1) for part in range(2)
        ]
        real = jnp.where(at_top, -(position == step).astype(jnp.float32), pieces[0])
        imag = jnp.where(at_top, 0.0, pieces[1])
        real_high, real_low = split(real)
        imag_high, imag_low = split(imag)
        for part in range(2):
            if part == 0:
                high = [-real_high, imag_high]
                low = [-real_low, imag_low]
            else:
                high = [-imag_high, -real_high]
                low = [-imag_low, -real_low]
            for index, piece in enumerate(high + high + low + [chosen, chosen]):
                right_ref[part, index * width : (index + 1) * width, lanes] = piece
        keep = (latest < 0) & (position[:1] >= width)
        keep_ref[:, lanes] = jnp.broadcast_to(keep.astype(jnp.float32), (8, span))


def prepare(pivot_col, top, old, corner, panel):
    columns = top.shape[0]
    slots, _, width, share = panel.shape
    rows = slots * share
    whole = pl.BlockSpec(memory_space=pltpu.VMEM)
    return pl.pallas_call(
        prepare_kernel,
        out_shape=(
            jax.ShapeDtypeStruct((2, columns, 4 * LANES), jnp.bfloat16),
            jax.ShapeDtypeStruct((2, 8 * width, rows), jnp.bfloat16),
            jax.ShapeDtypeStruct((8, rows), jnp.float32),
        ),
        in_specs=[whole] * 5,
        out_specs=(whole,) * 3,
        compiler_params=pltpu.CompilerParams(vmem_limit_bytes=12 * MIB),
    )(pivot_col, top, old, corner, panel)


def columns_held(matrix):
    rows = matrix.shape[2]
    span = largest_divisor(rows, 2 * LANES, LANES)
    return span * (rows // span * 5 // 14)


def update_kernel(held_steps, left_ref, right_ref, keep_ref, *refs):
    *sources, out_ref = refs
    columns = out_ref.shape[1]
    rows = pl.ds(pl.multiple_of(pl.program_id(1) * columns, 16), columns)
    keep = keep_ref[:1, :] > 0.5

    def apply(source):
        for part in range(2):
            product = jnp.dot(left_ref[part, rows, :], right_ref[part], preferred_element_type=jnp.float32)
            out_ref[part] = jnp.where(keep, source[part], 0.0) + product

    if held_steps == 0:
        apply(sources[0])
        return

    @pl.when(pl.program_id(0) < held_steps)
    def _():
        apply(sources[1])

    @pl.when(pl.program_id(0) >= held_steps)
    def _():
        apply(sources[0])


def update(left, right, keep, matrix, kept):
    _, columns, rows = matrix.shape
    span = largest_divisor(rows, 2 * LANES, LANES)
    held_steps = 0 if kept is None else kept.shape[2] // span
    chunk = largest_divisor(columns, 896, 16)
    parts = columns // chunk
    sources = [matrix]
    if kept is not None:
        sources.append(pltpu.with_memory_space_constraint(kept, pltpu.VMEM))
    source_specs = [
        pl.BlockSpec(
            (2, chunk, span), lambda j, i: (0, jnp.where(j < held_steps, 0, i), jnp.maximum(j, held_steps))
        ),
        pl.BlockSpec(
            (2, chunk, span),
            lambda j, i: (0, jnp.where(j < held_steps, i, parts - 1), jnp.minimum(j, held_steps - 1)),
        ),
    ]
    return pl.pallas_call(
        lambda *refs: update_kernel(held_steps, *refs),
        out_shape=jax.ShapeDtypeStruct(matrix.shape, jnp.float32),
        grid=(rows // span, parts),
        in_specs=[
            pl.BlockSpec(left.shape, lambda j, i: (0, 0, 0), pipeline_mode=pl.Buffered(1)),
            pl.BlockSpec((2, right.shape[1], span), lambda j, i: (0, 0, j)),
            pl.BlockSpec((8, span), lambda j, i: (0, j)),
        ] + source_specs[: len(sources)],
        out_specs=pl.BlockSpec((2, chunk, span), lambda j, i: (0, i, j)),
        compiler_params=pltpu.CompilerParams(vmem_limit_bytes=22 * MIB),
    )(left, right, keep, *sources)


def exchange_kernel(
    peers, ring, pivot_row_ref, pivot_col_ref, corner_ref, panel_ref, matrix_ref,
    top_ref, old_ref, corner_out_ref, slots_ref, kept_ref,
    choose, mine, old, inbox, total,
    rs_send, rs_recv, ag_send, ag_recv, old_send, old_recv, spread_send, spread_recv,
    panel_send, panel_recv, pass_send, pass_recv, corner_send, corner_recv, local_sem,
):
    width = pivot_col_ref.shape[0]
    _, chunk, row_count = matrix_ref.shape
    quarter = chunk // peers
    last = pl.num_programs(0) - 1
    step = pl.program_id(0)
    p = lax.axis_index("prow")
    q = lax.axis_index("pcol")
    sibling = q + 1 - 2 * lax.rem(q, 2)
    hops = ring // 2

    def other(d):
        return lax.rem(p + d, peers)

    def sender(d):
        return lax.rem(p + peers - d, peers)

    def along(d):
        return lax.rem(q + 2 * d, ring)

    def behind(d):
        return lax.rem(q + ring - 2 * d, ring)

    def remote(src, dst, send, recv, row, column):
        return pltpu.make_async_remote_copy(
            src_ref=src, dst_ref=dst, send_sem=send, recv_sem=recv,
            device_id=(row, column), device_id_type=pl.DeviceIdType.MESH,
        )

    def part_rows(i, owner):
        return pl.ds(pl.multiple_of(i * chunk + owner * quarter, quarter), quarter)

    def scatter_copy(i, d):
        return remote(
            mine.at[part_rows(i, other(d))], inbox.at[i, d - 1], rs_send.at[i, d - 1], rs_recv.at[i, d - 1], other(d), q
        )

    def gather_copy(i, d, owner):
        return remote(
            total.at[i], top_ref.at[part_rows(i, owner)], ag_send.at[i, d - 1], ag_recv.at[i, d - 1], other(d), q
        )

    def old_copy(i, d, target):
        return remote(
            old.at[part_rows(i, target)], old_ref.at[part_rows(i, target)], old_send.at[i, d - 1], old_recv.at[i], other(d), q
        )

    def spread_root(i, d):
        return remote(
            old.at[part_rows(i, 0)], old_ref.at[part_rows(i, 0)], spread_send.at[i, d - 1], spread_recv.at[i, d - 1], other(d), q
        )

    def spread_copy(i, d, owner):
        return remote(
            old_ref.at[part_rows(i, owner)], old_ref.at[part_rows(i, owner)],
            spread_send.at[i, d - 1], spread_recv.at[i, d - 1], other(d), q,
        )

    def panel_copy(d, owner):
        return remote(panel_ref, slots_ref.at[owner], panel_send.at[d], panel_recv.at[d], p, along(d))

    def sibling_copy():
        return remote(panel_ref, slots_ref.at[q], panel_send.at[0], panel_recv.at[0], p, sibling)

    def pass_copy(d, owner):
        return remote(slots_ref.at[owner], slots_ref.at[owner], pass_send.at[d], pass_recv.at[d], p, sibling)

    def corner_down(d):
        return remote(corner_ref, corner_out_ref, corner_send.at[d - 1], corner_recv.at[0], other(d), q)

    def corner_across(d):
        return remote(
            corner_ref, corner_out_ref, corner_send.at[peers + d - 1], corner_recv.at[0], p, lax.rem(q + d, ring)
        )

    def corner_forward(d):
        return remote(
            corner_out_ref, corner_out_ref, corner_send.at[peers + d - 1], corner_recv.at[0], p, lax.rem(q + d, ring)
        )

    def own_panel():
        return pltpu.make_async_copy(panel_ref, slots_ref.at[q], local_sem.at[0])

    def own_corner():
        return pltpu.make_async_copy(corner_ref, corner_out_ref, local_sem.at[1])

    def own_old():
        return pltpu.make_async_copy(old, old_ref, local_sem.at[2])

    def own_total(i):
        return pltpu.make_async_copy(total.at[i], top_ref.at[part_rows(i, p)], local_sem.at[3 + i])

    @pl.when(step == 0)
    def _():
        barrier = pltpu.get_barrier_semaphore()
        for d in range(1, peers):
            pl.semaphore_signal(barrier, inc=1, device_id=(other(d), q), device_id_type=pl.DeviceIdType.MESH)
        for d in range(1, ring):
            pl.semaphore_signal(
                barrier, inc=1, device_id=(p, lax.rem(q + d, ring)), device_id_type=pl.DeviceIdType.MESH
            )
        pl.semaphore_wait(barrier, peers + ring - 2)
        for d in range(1, hops):
            panel_copy(d, q).start()
        sibling_copy().start()
        own_panel().start()

        @pl.when((p == 0) & (q == 0))
        def _():
            for d in range(1, peers):
                corner_down(d).start()
            for d in range(1, ring):
                corner_across(d).start()
            own_corner().start()

        wanted = wanted_rows(pivot_row_ref[...], pivot_col_ref[...])[:1] - p * row_count
        wanted = jnp.concatenate([wanted[:, :width], wanted[:, :width]], axis=1)
        row = lax.broadcasted_iota(jnp.int32, choose.shape, 0)
        choose[...] = (row == wanted).astype(jnp.float32).astype(jnp.bfloat16)

    here = pl.ds(pl.multiple_of(step * chunk, chunk), chunk)
    held = kept_ref.shape[2]
    keep_copy = pltpu.make_async_copy(
        matrix_ref.at[:, :, pl.ds(0, held)], kept_ref.at[:, here, :], local_sem.at[3 + last + 1]
    )
    keep_copy.start()
    found = []
    for part in range(2):
        high, low = split(matrix_ref[part])
        found.append(
            jnp.dot(high, choose[...], preferred_element_type=jnp.float32)
            + jnp.dot(low, choose[...], preferred_element_type=jnp.float32)
        )
    lane = lax.broadcasted_iota(jnp.int32, (chunk, LANES), 1)
    mine[here, :] = jnp.where(lane < width, found[0], found[1])
    for d in range(1, peers):
        scatter_copy(step, d).start()

    @pl.when(p == 0)
    def _():
        old[here, :] = jnp.concatenate([matrix_ref[0, :, :width], matrix_ref[1, :, :width]], axis=1)
        for d in range(1, peers):
            old_copy(step, d, d).start()
        for d in range(1, peers):
            spread_root(step, d).start()

    def finish(i):
        for d in range(1, peers):
            scatter_copy(i, d).wait_recv()
        summed = mine[part_rows(i, p), :]
        for d in range(1, peers):
            summed = summed + inbox[i, d - 1]
        total[i] = summed
        for d in range(1, peers):
            gather_copy(i, d, p).start()
        own_total(i).start()

        @pl.when(p != 0)
        def _():
            old_copy(i, 1, p).wait_recv()
            for d in range(1, peers):
                @pl.when(other(d) != 0)
                def _(d=d):
                    spread_copy(i, d, p).start()

    @pl.when(step > 0)
    def _():
        finish(step - 1)

    keep_copy.wait()

    @pl.when(step == last)
    def _():
        for d in range(1, hops):
            panel_copy(d, behind(d)).wait_recv()
            pass_copy(d, behind(d)).start()

        @pl.when((q == 0) & (p != 0))
        def _():
            corner_down(1).wait_recv()
            for d in range(1, ring):
                corner_forward(d).start()

        finish(last)

        @pl.when(p == 0)
        def _():
            own_old().start()
            own_old().wait()

        @pl.when((p == 0) & (q == 0))
        def _():
            own_corner().wait()
            for d in range(1, peers):
                corner_down(d).wait_send()
            for d in range(1, ring):
                corner_across(d).wait_send()

        @pl.when((p != 0) & (q == 0))
        def _():
            for d in range(1, ring):
                corner_forward(d).wait_send()

        @pl.when(q != 0)
        def _():
            corner_across(1).wait_recv()

        own_panel().wait()
        remote(panel_ref, slots_ref.at[sibling], panel_send.at[0], panel_recv.at[0], p, sibling).wait()
        for d in range(1, hops):
            panel_copy(d, q).wait_send()
            pass_copy(d, behind(d)).wait_send()
            pass_copy(d, lax.rem(sibling + ring - 2 * d, ring)).wait_recv()

        def drain(i, carry):
            own_total(i).wait()
            for d in range(1, peers):
                scatter_copy(i, d).wait_send()
                gather_copy(i, d, p).wait_send()
                gather_copy(i, d, sender(d)).wait_recv()

            @pl.when(p == 0)
            def _():
                for d in range(1, peers):
                    old_copy(i, d, d).wait_send()
                    spread_root(i, d).wait_send()

            @pl.when(p != 0)
            def _():
                for d in range(1, peers):
                    spread_copy(i, d, sender(d)).wait_recv()

                    @pl.when(other(d) != 0)
                    def _(d=d):
                        spread_copy(i, d, p).wait_send()

            return carry

        lax.fori_loop(0, last + 1, drain, 0)


def exchange(pivot_row, pivot_col, corner, panel, matrix, chunk, held):
    _, columns, rows = matrix.shape
    peers, ring = lax.axis_size("prow"), lax.axis_size("pcol")
    steps = columns // chunk
    quarter = chunk // peers
    anywhere = pl.BlockSpec(memory_space=pl.ANY)
    dma = pltpu.SemaphoreType.DMA
    return pl.pallas_call(
        lambda *refs: exchange_kernel(peers, ring, *refs),
        out_shape=(
            jax.ShapeDtypeStruct((columns, LANES), jnp.float32),
            jax.ShapeDtypeStruct((columns, LANES), jnp.float32),
            jax.ShapeDtypeStruct(corner.shape, jnp.float32),
            jax.ShapeDtypeStruct((ring,) + panel.shape, jnp.float32),
            pltpu.VMEM((2, columns, held), jnp.float32),
        ),
        grid=(steps,),
        in_specs=[
            pl.BlockSpec(pivot_row.shape, lambda i: (0, 0)),
            pl.BlockSpec(pivot_col.shape, lambda i: (0, 0)),
            anywhere,
            anywhere,
            pl.BlockSpec((2, chunk, rows), lambda i: (0, i, 0)),
        ],
        out_specs=(anywhere,) * 5,
        scratch_shapes=[
            pltpu.VMEM((rows, LANES), jnp.bfloat16),
            pltpu.VMEM((columns, LANES), jnp.float32),
            pltpu.VMEM((columns, LANES), jnp.float32),
            pltpu.VMEM((steps, peers - 1, quarter, LANES), jnp.float32),
            pltpu.VMEM((steps, quarter, LANES), jnp.float32),
            dma((steps, peers - 1)), dma((steps, peers - 1)),
            dma((steps, peers - 1)), dma((steps, peers - 1)),
            dma((steps, peers - 1)), dma((steps,)),
            dma((steps, peers - 1)), dma((steps, peers - 1)),
            dma((ring // 2,)), dma((ring // 2,)),
            dma((ring // 2,)), dma((ring // 2,)),
            dma((peers + ring,)), dma((1,)), dma((4 + steps,)),
        ],
        compiler_params=pltpu.CompilerParams(
            vmem_limit_bytes=34 * MIB, collective_id=0, has_side_effects=True
        ),
        cost_estimate=pl.CostEstimate(flops=columns * rows * 8 * LANES, bytes_accessed=columns * rows * 8, transcendentals=0),
    )(pivot_row, pivot_col, corner, panel, matrix)


def exchange_plain(pivot_row, pivot_col, corner, panel, matrix):
    width = panel.shape[1]
    slots = lax.all_gather(panel, "pcol")
    mine = (lax.axis_index("prow") == 0) & (lax.axis_index("pcol") == 0)
    share = panel.shape[2]
    if share < width:
        head = jnp.concatenate([slots[k] for k in range(-(-width // share))], axis=2)[:, :, :width]
        first = jnp.where(lax.axis_index("prow") == 0, head, 0.0)
        corner = lax.psum(first, "prow")
    else:
        corner = lax.psum(jnp.where(mine, panel[:, :, :width], 0.0), ("prow", "pcol"))
    corner = jnp.concatenate([corner[0], corner[1]], axis=1)
    slab = lax.psum(pick(pivot_row, pivot_col, matrix), "prow")
    top = jnp.concatenate([slab[0, :, :width], slab[1, :, :width]], axis=1)
    old = jnp.concatenate([slab[0, :, width:], slab[1, :, width:]], axis=1)
    slots = jnp.moveaxis(slots, 0, 2).reshape(1, 2, width, -1)
    return top, old, corner, slots


def on_device(matrix, panel_lower, pivot_rows):
    width = pivot_rows.shape[0]
    share = panel_lower.shape[2]
    columns = matrix.shape[1]
    peers, ring = lax.axis_size("prow"), lax.axis_size("pcol")
    pivot_row = jnp.pad(pivot_rows, (0, LANES - width), constant_values=-1).reshape(1, LANES)
    pivot_col = pivot_rows.reshape(width, 1)
    chunk = largest_divisor(columns, 256, 16)
    if share % width == 0 and ring <= 8 and chunk % (8 * peers) == 0:
        corner = jnp.concatenate([panel_lower[0, :, :width], panel_lower[1, :, :width]], axis=1)
        *moved, kept = exchange(pivot_row, pivot_col, corner, panel_lower, matrix, chunk, columns_held(matrix))
    else:
        moved, kept = exchange_plain(pivot_row, pivot_col, None, panel_lower, matrix), None
    left, right, keep = prepare(pivot_col, *moved)
    return update(left, right, keep, matrix, kept)


def solution(mesh):
    return jax.shard_map(
        on_device,
        mesh=mesh,
        in_specs=(P(None, "pcol", "prow"), P(None, None, ("prow", "pcol")), P()),
        out_specs=P(None, "pcol", "prow"),
        check_vma=False,
    )
```
